32 devices in a mesh: wide: 8 (over y, x, core), blk: 4 (over z).
Axes of the slice: x: 2, y: 2, z: 4, core: 2. Of those that a mesh axis runs over, the one named last changes fastest.
Arguments:
- tokens: bfloat16 [512, 8192], P('wide', 'blk'), may hold values from -6 to 6
- target: bfloat16 [512, 8192], P('wide', 'blk'), may hold values from -3 to 3
- probe_vector: float32 [8192], P('blk'), may hold values from -12 to 12
- weight_in: bfloat16 [256, 4, 2, 128, 128], P('wide', 'blk'), may hold values from -0.375 to 0.375
- weight_out: bfloat16 [256, 4, 2, 128, 128], P('wide', 'blk'), may hold values from -0.09375 to 0.09375
- slot_rows: int32 [256, 4, 2], P('wide', 'blk'), may hold values from 0 to 15, as said below
- slot_count: int32 [256, 4], P('wide', 'blk'), may hold values from 0 to 2, as said below
Outputs:
- outputs: bfloat16 [512, 8192], P('wide', 'blk')
- token_grad: bfloat16 [512, 8192], P('wide', 'blk')
- grad_in: float32 [256, 4, 2, 128, 128], P('wide', 'blk')
- grad_out: float32 [256, 4, 2, 128, 128], P('wide', 'blk')
The draws below stay inside these ranges and needn't reach their ends.
Inputs may be any that keep to these rules, and one draw needn't show every extreme that they name: `slot_rows`: the 2 entries of one (j, g) are distinct feature blocks of the row group. `slot_count`: every hidden block column has 2 used slots in at least one row group.
All inputs are finite; a program needn't handle non-finite values.
Results may differ from the reference program's by a relative error of at most 0.033.
Values may be sent and summed in bfloat16 or wider, within the bound.
A program may use at most 128 MiB of HBM per device.

```python
import jax
import jax.numpy as jnp
from jax import lax

D = 8192
H = 32768
BLK = 128
CAP = 2
TOKENS = 512
HB = 256
RG = 4
RBG = 16
N_WIDE = 8


def draw_probe_vector(key, part):
    position = jnp.arange(D, dtype=jnp.float32) / max(D - 1, 1)
    rising = 1.0 + 2.0 * position
    base = jnp.clip(jax.random.normal(key, (D,), jnp.float32), -4.0, 4.0)
    return base * rising


def draw_weight_in(key, part):
    shape = (HB, RG, CAP, BLK, BLK)
    column = jnp.arange(HB, dtype=jnp.float32).reshape(HB, 1, 1, 1, 1) / max(HB - 1, 1)
    rising = (1.0 + 2.0 * column) / (D // 8) ** 0.5
    base = jnp.clip(jax.random.normal(key, shape, jnp.float32), -4.0, 4.0)
    return (base * rising).astype(jnp.bfloat16)


def draw_slot_rows(key, part):
    scores = jax.random.randint(key, (HB, RG, RBG), 0, 1 << 20) * RBG + jnp.arange(RBG, dtype=jnp.int32)
    order = jnp.argsort(scores, axis=-1)
    return order[:, :, :CAP].astype(jnp.int32)


def draw_slot_count(key, part):
    first_key, second_key = jax.random.split(key)
    levels = jax.random.randint(first_key, (HB, RG), 0, CAP + 1)
    filled = jax.random.randint(second_key, (HB, 1), 0, RG)
    groups = jnp.arange(RG, dtype=jnp.int32)[None, :]
    return jnp.where(groups == filled, CAP, levels).astype(jnp.int32)


def shard_levels(own_key, extent, cuts, low, high):
    def one(dim, blocks):
        draws = jax.random.uniform(jax.random.fold_in(jax.random.fold_in(own_key, 6), dim), (blocks,), jnp.float32, low / len(cuts), high / len(cuts))
        return jnp.repeat(jnp.exp(draws), extent[dim] // blocks).reshape((-1,) + (1,) * (len(extent) - dim - 1))

    gain = one(*cuts[0])
    for cut in cuts[1:]:
        gain = gain * one(*cut)
    return gain


def centred(own_key, dims, scale, reach, cuts=(), kind=jnp.bfloat16):
    values = jax.random.normal(own_key, dims, jnp.float32) * scale
    if len(cuts) > 0:
        values = shard_levels(own_key, dims, cuts, -0.22, 0.18) * values
    return jnp.clip(values, min=-reach, max=reach).astype(kind)


def setup_inputs(seed: int = 0) -> dict:
    arg_keys = jax.random.split(jax.random.key(seed), 8)
    return {
        "tokens": centred(arg_keys[0], (TOKENS, D), 1.0, 6.0, ((0, 8), (1, 4))),
        "target": centred(arg_keys[1], (TOKENS, D), 0.5, 3.0, ((0, 8), (1, 4))),
        "probe_vector": draw_probe_vector(jax.random.fold_in(arg_keys[7], 71), 0),
        "weight_in": draw_weight_in(jax.random.fold_in(arg_keys[7], 71), 0),
        "weight_out": centred(arg_keys[4], (HB, RG, CAP, BLK, BLK), (H // 8) ** -0.5, 0.09375, ((0, 8), (1, 4))),
        "slot_rows": draw_slot_rows(jax.random.fold_in(arg_keys[7], 71), 0),
        "slot_count": draw_slot_count(jax.random.fold_in(arg_keys[7], 71), 0),
    }


def activate(value):
    return jax.nn.gelu(value, approximate=True)

def activate_slope(value):
    return jax.jvp(activate, (value,), (jnp.ones_like(value),))[1]

def rounded(value):
    lowered = lax.optimization_barrier(value.astype(jnp.bfloat16))
    return lowered.astype(jnp.float32)

def pick_rows(blocks, row_index):
    group = lax.broadcasted_iota(jnp.int32, row_index.shape, 1)
    return blocks[:, group, row_index, :]

def place_rows(contrib, row_index):
    onehot = (row_index[..., None] == lax.broadcasted_iota(jnp.int32, row_index.shape + (RBG,), 3)).astype(jnp.float32)
    placed = jnp.einsum('tjgsn,jgsr->tgrn', contrib, onehot)
    return placed.reshape(contrib.shape[0], D)

def reference(tokens, target, probe_vector, weight_in, weight_out, slot_rows, slot_count):
    in_use = lax.broadcasted_iota(jnp.int32, slot_rows.shape, 2) < slot_count[:, :, None]
    mask = in_use.astype(jnp.float32)[..., None, None]
    tiles_in = weight_in.astype(jnp.float32) * mask
    tiles_out = weight_out.astype(jnp.float32) * mask
    inputs = tokens.astype(jnp.float32).reshape(TOKENS, RG, RBG, BLK)
    chosen = pick_rows(probe_vector.reshape(1, RG, RBG, BLK), slot_rows)[0]
    image = jnp.einsum('jgsk,jgskn->jn', chosen, tiles_in, precision=lax.Precision.HIGHEST)
    norm_probe = jnp.sum(probe_vector * probe_vector)
    spectral = jnp.sqrt(jnp.sum(image * image) / norm_probe)
    per_group = HB // N_WIDE

    def grouped(array):
        return array.reshape((N_WIDE, per_group) + array.shape[1:])
    items = (grouped(tiles_in), grouped(tiles_out), grouped(slot_rows))

    def hidden_of(tile_group, row_group):
        picked = pick_rows(inputs, row_group)
        return jnp.einsum('tjgsk,jgskn->tjn', picked, tile_group) / spectral

    def forward_group(carry, item):
        tile_group, out_group, row_group = item
        hidden = hidden_of(tile_group, row_group)
        active = rounded(activate(hidden))
        contrib = jnp.einsum('tjk,jgskn->tjgsn', active, out_group)
        return (carry + rounded(place_rows(contrib, row_group)), None)
    summed, unused = lax.scan(forward_group, jnp.zeros((TOKENS, D), jnp.float32), items)
    outputs = summed.astype(jnp.bfloat16)
    residual = (outputs.astype(jnp.float32) - target.astype(jnp.float32)).astype(jnp.bfloat16)
    errors = residual.astype(jnp.float32).reshape(TOKENS, RG, RBG, BLK)

    def backward_group(carry, item):
        tile_group, out_group, row_group = item
        hidden = hidden_of(tile_group, row_group)
        active = rounded(activate(hidden))
        picked_err = pick_rows(errors, row_group)
        back = jnp.einsum('tjgsn,jgskn->tjk', picked_err, out_group)
        slope = rounded(back * activate_slope(hidden))
        part_out = jnp.einsum('tjk,tjgsn->jgskn', active, picked_err)
        picked_in = pick_rows(inputs, row_group)
        part_in = jnp.einsum('tjgsk,tjn->jgskn', picked_in, slope)
        spread = jnp.einsum('tjn,jgskn->tjgsk', slope, tile_group)
        return (carry + rounded(place_rows(spread, row_group)), (part_in, part_out))
    back_sum, stacked = lax.scan(backward_group, jnp.zeros((TOKENS, D), jnp.float32), items)
    raw_in = stacked[0].reshape(HB, RG, CAP, BLK, BLK) * mask
    grad_out = stacked[1].reshape(HB, RG, CAP, BLK, BLK) * mask
    curvature = jnp.sum(raw_in * tiles_in)
    outer = jnp.einsum('jgsk,jn->jgskn', chosen, image) * mask
    grad_in = raw_in / spectral - curvature / (spectral ** 3 * norm_probe) * outer
    token_grad = (back_sum / spectral).astype(jnp.bfloat16)
    return (outputs, token_grad, grad_in, grad_out)
```

```python
import functools
import math

import jax
import jax.numpy as jnp
from jax import lax
from jax.experimental import pallas as pl
from jax.experimental.pallas import tpu as pltpu
from jax.sharding import PartitionSpec as P

MESH = pl.DeviceIdType.MESH
RATE = math.sqrt(2.0 / math.pi)
CUBIC = 0.044715
LAG = 2
RING = 3
VMEM_LIMIT = 48 * 1024 * 1024


def expand_kernel(block, rows_ref, count_ref, win_ref, wout_ref, w1_ref, w2_ref):
    chunk = pl.program_id(0)
    per, _, slots = win_ref.shape[:3]
    w1_ref[...] = jnp.zeros_like(w1_ref)
    w2_ref[...] = jnp.zeros_like(w2_ref)
    for j in range(per):
        column = chunk * per + j
        for s in range(slots):
            used = s < count_ref[column]
            at = pl.ds(pl.multiple_of(rows_ref[column * slots + s] * block, block), block)
            here = slice(j * block, (j + 1) * block)
            tile_in = win_ref[j, 0, s]
            tile_out = wout_ref[j, 0, s]
            w1_ref[0, at, here] = jnp.where(used, tile_in, jnp.zeros_like(tile_in))
            w2_ref[0, here, at] = jnp.where(used, tile_out, jnp.zeros_like(tile_out))


def expand(rows, counts, weight_in, weight_out, features, per):
    columns, _, slots, block, _ = weight_in.shape
    width = per * block
    chunks = columns // per
    tile_spec = pl.BlockSpec((per, 1, slots, block, block), lambda c, *_: (c, 0, 0, 0, 0))
    return pl.pallas_call(
        functools.partial(expand_kernel, block),
        grid_spec=pltpu.PrefetchScalarGridSpec(
            num_scalar_prefetch=2,
            grid=(chunks,),
            in_specs=[tile_spec, tile_spec],
            out_specs=[
                pl.BlockSpec((1, features, width), lambda c, *_: (c, 0, 0)),
                pl.BlockSpec((1, width, features), lambda c, *_: (c, 0, 0)),
            ],
        ),
        out_shape=[
            jax.ShapeDtypeStruct((chunks, features, width), jnp.bfloat16),
            jax.ShapeDtypeStruct((chunks, width, features), jnp.bfloat16),
        ],
        compiler_params=pltpu.CompilerParams(vmem_limit_bytes=VMEM_LIMIT),
        cost_estimate=pl.CostEstimate(
            flops=0, bytes_accessed=chunks * width * features * 5, transcendentals=0
        ),
        name="expand_tiles",
    )(rows, counts, weight_in, weight_out)


def line_sum_loop(
    n, chunks, own_of, finish, own, to_right, to_left, from_left, from_right, sems, panels
):
    right_sent, left_sent, left_came, right_came = sems
    first_hbm, first_buf, first_sem, last_hbm, last_buf, last_sem = panels
    me = lax.axis_index("blk")
    right = jnp.minimum(me + 1, n - 1)
    left = jnp.maximum(me - 1, 0)

    def right_copy(c):
        return pltpu.make_async_remote_copy(
            src_ref=to_right.at[c],
            dst_ref=from_left.at[c],
            send_sem=right_sent.at[c],
            recv_sem=left_came.at[c],
            device_id={"blk": right},
            device_id_type=MESH,
        )

    def left_copy(c):
        return pltpu.make_async_remote_copy(
            src_ref=to_left.at[c],
            dst_ref=from_right.at[c],
            send_sem=left_sent.at[c],
            recv_sem=right_came.at[c],
            device_id={"blk": left},
            device_id_type=MESH,
        )

    def first_copy(c):
        slot = lax.rem(c, RING)
        return pltpu.make_async_copy(first_hbm.at[c], first_buf.at[slot], first_sem.at[slot])

    def last_copy(c):
        slot = lax.rem(c, RING)
        return pltpu.make_async_copy(last_hbm.at[c], last_buf.at[slot], last_sem.at[slot])

    for c in range(min(RING, chunks)):
        first_copy(jnp.int32(c)).start()
        last_copy(jnp.int32(c)).start()

    @pl.when(me == 0)
    def _():
        from_left[...] = jnp.zeros_like(from_left)

    @pl.when(me == n - 1)
    def _():
        from_right[...] = jnp.zeros_like(from_right)

    barrier = pltpu.get_barrier_semaphore()

    @pl.when(me > 0)
    def _():
        pl.semaphore_signal(barrier, inc=1, device_id={"blk": left}, device_id_type=MESH)

    @pl.when(me < n - 1)
    def _():
        pl.semaphore_signal(barrier, inc=1, device_id={"blk": right}, device_id_type=MESH)

    peers = jnp.where(me > 0, 1, 0) + jnp.where(me < n - 1, 1, 0)
    pl.semaphore_wait(barrier, peers)

    def step(t, carry):
        @pl.when(t < chunks)
        def _():
            first_copy(t).wait()
            own[t] = own_of(first_buf[lax.rem(t, RING)])

            @pl.when(t + RING < chunks)
            def _():
                first_copy(t + RING).start()

        onward = t - LAG * me

        @pl.when((onward >= 0) & (onward < chunks))
        def _():
            @pl.when(me > 0)
            def _():
                right_copy(onward).wait_recv()

            @pl.when(me < n - 1)
            def _():
                to_right[onward] = (
                    own[onward] + from_left[onward].astype(jnp.float32)
                ).astype(jnp.bfloat16)
                right_copy(onward).start()

        back = t - LAG * (n - 1 - me)

        @pl.when((back >= 0) & (back < chunks))
        def _():
            @pl.when(me < n - 1)
            def _():
                left_copy(back).wait_recv()

            @pl.when(me > 0)
            def _():
                to_left[back] = (
                    own[back] + from_right[back].astype(jnp.float32)
                ).astype(jnp.bfloat16)
                left_copy(back).start()

        done = t - LAG * (n - 1)

        @pl.when(done >= 0)
        def _():
            last_copy(done).wait()
            total = (
                own[done]
                + from_left[done].astype(jnp.float32)
                + from_right[done].astype(jnp.float32)
            )
            finish(done, total, last_buf[lax.rem(done, RING)])

            @pl.when(done + RING < chunks)
            def _():
                last_copy(done + RING).start()

        return carry

    lax.fori_loop(0, chunks + LAG * (n - 1), step, 0)

    def drain(c, carry):
        @pl.when(me < n - 1)
        def _():
            right_copy(c).wait_send()

        @pl.when(me > 0)
        def _():
            left_copy(c).wait_send()

        return carry

    lax.fori_loop(0, chunks, drain, 0)


NT = (((1,), (1,)), ((), ()))


def forward_kernel(
    n, inv_ref, x_ref, w1_hbm, w2_hbm, out_ref, hidden_ref, active_ref,
    acc, own, to_right, to_left, from_left, from_right, s0, s1, s2, s3, b1, m1, b2, m2,
):
    chunks = w1_hbm.shape[0]
    acc[...] = jnp.zeros_like(acc)

    def own_of(panel):
        return jnp.dot(x_ref[...], panel, preferred_element_type=jnp.float32)

    def finish(c, total, panel):
        value = total * inv_ref[0, 0]
        curve = jnp.tanh(RATE * (value + CUBIC * value * value * value))
        active = (0.5 * value * (1.0 + curve)).astype(jnp.bfloat16)
        hidden_ref[c] = value.astype(jnp.bfloat16)
        active_ref[c] = active
        acc[...] += jnp.dot(active, panel, preferred_element_type=jnp.float32)

    line_sum_loop(
        n, chunks, own_of, finish, own, to_right, to_left, from_left, from_right,
        (s0, s1, s2, s3), (w1_hbm, b1, m1, w2_hbm, b2, m2),
    )
    out_ref[...] = acc[...].astype(jnp.bfloat16)


def backward_kernel(
    n, e_ref, hidden_ref, w2_hbm, w1_hbm, out_ref, slope_ref, curv_ref,
    acc, own, to_right, to_left, from_left, from_right, s0, s1, s2, s3, b1, m1, b2, m2,
):
    chunks = w1_hbm.shape[0]
    acc[...] = jnp.zeros_like(acc)
    curv_ref[...] = jnp.zeros_like(curv_ref)

    def own_of(panel):
        return lax.dot_general(e_ref[...], panel, NT, preferred_element_type=jnp.float32)

    def finish(c, total, panel):
        value = hidden_ref[c].astype(jnp.float32)
        square = value * value
        curve = jnp.tanh(RATE * (value + CUBIC * value * square))
        rise = 0.5 * (1.0 + curve) + 0.5 * value * (1.0 - curve * curve) * (
            RATE * (1.0 + 3.0 * CUBIC * square)
        )
        wide_slope = total * rise
        slope = wide_slope.astype(jnp.bfloat16)
        slope_ref[c] = slope
        rows, cols = value.shape
        curv_ref[...] += jnp.sum((wide_slope * value).reshape(rows // 8, 8, cols), axis=0)
        acc[...] += lax.dot_general(slope, panel, NT, preferred_element_type=jnp.float32)

    line_sum_loop(
        n, chunks, own_of, finish, own, to_right, to_left, from_left, from_right,
        (s0, s1, s2, s3), (w2_hbm, b1, m1, w1_hbm, b2, m2),
    )
    out_ref[...] = acc[...].astype(jnp.bfloat16)


def scratch_for(chunks, rows, width, features, first, last):
    moved = pltpu.VMEM((chunks, rows, width), jnp.bfloat16)
    return [
        pltpu.VMEM((rows, features), jnp.float32),
        pltpu.VMEM((chunks, rows, width), jnp.float32),
        moved, moved, moved, moved,
        *[pltpu.SemaphoreType.DMA((chunks,)) for _ in range(4)],
        pltpu.VMEM((RING,) + first, jnp.bfloat16),
        pltpu.SemaphoreType.DMA((RING,)),
        pltpu.VMEM((RING,) + last, jnp.bfloat16),
        pltpu.SemaphoreType.DMA((RING,)),
    ]


def line_cost(chunks, rows, width, features):
    return pl.CostEstimate(
        flops=chunks * width * features * rows * 4 * 8,
        bytes_accessed=chunks * width * features * 4,
        transcendentals=chunks * rows * width,
    )


VM = pl.BlockSpec(memory_space=pltpu.VMEM)
ANY = pl.BlockSpec(memory_space=pl.ANY)


def forward_half(n, inv, x, w1, w2, ident):
    chunks, features, width = w1.shape
    rows = x.shape[0]
    kept = jax.ShapeDtypeStruct((chunks, rows, width), jnp.bfloat16)
    return pl.pallas_call(
        functools.partial(forward_kernel, n),
        out_shape=[jax.ShapeDtypeStruct((rows, features), jnp.bfloat16), kept, kept],
        in_specs=[pl.BlockSpec(memory_space=pltpu.SMEM), VM, ANY, ANY],
        out_specs=[VM, VM, VM],
        scratch_shapes=scratch_for(
            chunks, rows, width, features, (features, width), (width, features)
        ),
        compiler_params=pltpu.CompilerParams(
            collective_id=ident, has_side_effects=True, vmem_limit_bytes=VMEM_LIMIT
        ),
        cost_estimate=line_cost(chunks, rows, width, features),
        name="forward_half_" + "ab"[ident],
    )(inv, x, w1, w2)


def backward_half(n, err, hidden, w2, w1, ident):
    chunks, features, width = w1.shape
    rows = err.shape[0]
    return pl.pallas_call(
        functools.partial(backward_kernel, n),
        out_shape=[
            jax.ShapeDtypeStruct((rows, features), jnp.bfloat16),
            jax.ShapeDtypeStruct((chunks, rows, width), jnp.bfloat16),
            jax.ShapeDtypeStruct((8, width), jnp.float32),
        ],
        in_specs=[VM, VM, ANY, ANY],
        out_specs=[VM, VM, VM],
        scratch_shapes=scratch_for(
            chunks, rows, width, features, (width, features), (features, width)
        ),
        compiler_params=pltpu.CompilerParams(
            collective_id=2 + ident, has_side_effects=True, vmem_limit_bytes=VMEM_LIMIT
        ),
        cost_estimate=line_cost(chunks, rows, width, features),
        name="backward_half_" + "ab"[ident],
    )(err, hidden, w2, w1)


TN = (((0,), (0,)), ((), ()))


def tile_grad_kernel(block, picked_first, rows_ref, count_ref, fa_ref, fb_ref, ha_ref, hb_ref, out_ref):
    chunk = pl.program_id(0)
    per, _, slots = out_ref.shape[:3]
    for j in range(per):
        column = chunk * per + j
        here = slice(j * block, (j + 1) * block)
        hidden_a = ha_ref[0, :, here]
        hidden_b = hb_ref[0, :, here]
        for s in range(slots):
            used = s < count_ref[column]
            at = pl.ds(pl.multiple_of(rows_ref[column * slots + s] * block, block), block)
            pick_a = fa_ref[:, at]
            pick_b = fb_ref[:, at]
            pairs = ((pick_a, hidden_a), (pick_b, hidden_b))
            total = 0.0
            for pick, hid in pairs:
                ends = (pick, hid) if picked_first else (hid, pick)
                total = total + lax.dot_general(*ends, TN, preferred_element_type=jnp.float32)
            out_ref[j, 0, s] = jnp.where(used, total, jnp.zeros_like(total))


def tile_grad(rows, counts, feat_a, feat_b, hid_a, hid_b, shape, picked_first, name):
    columns, _, slots, block, _ = shape
    chunks, _, width = hid_a.shape
    per = width // block
    whole = pl.BlockSpec(feat_a.shape, lambda c, *_: (0, 0))
    part = pl.BlockSpec((1,) + hid_a.shape[1:], lambda c, *_: (c, 0, 0))
    return pl.pallas_call(
        functools.partial(tile_grad_kernel, block, picked_first),
        grid_spec=pltpu.PrefetchScalarGridSpec(
            num_scalar_prefetch=2,
            grid=(chunks,),
            in_specs=[whole, whole, part, part],
            out_specs=pl.BlockSpec((per, 1, slots, block, block), lambda c, *_: (c, 0, 0, 0, 0)),
        ),
        out_shape=jax.ShapeDtypeStruct(shape, jnp.float32),
        compiler_params=pltpu.CompilerParams(vmem_limit_bytes=VMEM_LIMIT),
        cost_estimate=pl.CostEstimate(
            flops=columns * slots * block * block * feat_a.shape[0] * 4 * 8,
            bytes_accessed=columns * slots * block * block * 12,
            transcendentals=0,
        ),
        name=name,
    )(rows, counts, feat_a, feat_b, hid_a, hid_b)


def body(n, tokens, target, probe_vector, weight_in, weight_out, slot_rows, slot_count):
    columns, unit, slots, block, width_two = weight_in.shape
    owned, features = tokens.shape
    feature_blocks = features // block
    per = 2
    half = owned // 2
    row_index = slot_rows[:, 0]
    flat_rows = row_index.reshape(-1)
    flat_count = slot_count.reshape(-1)

    def gather(piece):
        return lax.all_gather(piece, "wide", axis=0, tiled=True)

    def scatter(piece):
        return lax.psum_scatter(piece, "wide", scatter_dimension=0, tiled=True)

    x_a = gather(tokens[:half])
    x_b = gather(tokens[half:])

    in_use = lax.broadcasted_iota(jnp.int32, (columns, slots), 1) < slot_count[:, 0][:, None]
    mask_low = in_use.astype(jnp.bfloat16)[:, :, None, None]
    mask_full = in_use.astype(jnp.float32)[:, :, None, None]
    tiles_in = weight_in[:, 0] * mask_low
    chosen = jnp.take(probe_vector.reshape(feature_blocks, block), flat_rows, axis=0).reshape(
        columns, slots, block
    )
    image_part = jnp.einsum(
        "jsk,jskn->jn", chosen, tiles_in.astype(jnp.float32), precision=lax.Precision.HIGHEST
    )
    image, norm_probe = lax.psum((image_part, jnp.sum(probe_vector * probe_vector)), "blk")
    norm_image = lax.psum(jnp.sum(image * image), "wide")
    spectral = jnp.sqrt(norm_image / norm_probe)
    inverse = (1.0 / spectral).reshape(1, 1)

    w1, w2 = expand(flat_rows, flat_count, weight_in, weight_out, features, per)

    part_a, hidden_a, active_a = forward_half(n, inverse, x_a, w1, w2, 0)
    out_a = scatter(part_a)
    part_b, hidden_b, active_b = forward_half(n, inverse, x_b, w1, w2, 1)
    err_a = gather(residual_of(out_a, target[:half]))
    out_b = scatter(part_b)
    back_a, slope_a, curv_a = backward_half(n, err_a, hidden_a, w2, w1, 0)
    err_b = gather(residual_of(out_b, target[half:]))
    grad_a = scatter(back_a)
    back_b, slope_b, curv_b = backward_half(n, err_b, hidden_b, w2, w1, 1)
    grad_b = scatter(back_b)
    curvature = spectral * lax.psum(jnp.sum(curv_a + curv_b), "wide")
    grad_out = tile_grad(
        flat_rows, flat_count, err_a, err_b, active_a, active_b, weight_out.shape, False, "grad_out"
    )
    raw_in = tile_grad(
        flat_rows, flat_count, x_a, x_b, slope_a, slope_b, weight_in.shape, True, "raw_in"
    )
    outer = jnp.einsum("jsk,jn->jskn", chosen, image) * mask_full
    grad_in = raw_in / spectral - (curvature / (spectral**3 * norm_probe) * outer)[:, None]
    outputs = jnp.concatenate([out_a, out_b], axis=0)
    token_grad = (
        jnp.concatenate([grad_a, grad_b], axis=0).astype(jnp.float32) / spectral
    ).astype(jnp.bfloat16)
    return (outputs, token_grad, grad_in, grad_out)


def residual_of(outputs, target):
    return (outputs.astype(jnp.float32) - target.astype(jnp.float32)).astype(jnp.bfloat16)


def solution(mesh):
    in_specs = (
        P("wide", "blk"),
        P("wide", "blk"),
        P("blk"),
        P("wide", "blk", None, None, None),
        P("wide", "blk", None, None, None),
        P("wide", "blk", None),
        P("wide", "blk"),
    )
    out_specs = (
        P("wide", "blk"),
        P("wide", "blk"),
        P("wide", "blk", None, None, None),
        P("wide", "blk", None, None, None),
    )
    return jax.shard_map(
        functools.partial(body, mesh.shape["blk"]),
        mesh=mesh,
        in_specs=in_specs,
        out_specs=out_specs,
        check_vma=False,
    )
```

```python
import functools
import math

import jax
import jax.numpy as jnp
from jax import lax
from jax.experimental import pallas as pl
from jax.experimental.pallas import tpu as pltpu
from jax.sharding import PartitionSpec as P

MESH = pl.DeviceIdType.MESH
RATE = math.sqrt(2.0 / math.pi)
CUBIC = 0.044715
LAG = 2
RING = 3
VMEM_LIMIT = 48 * 1024 * 1024


def expand_kernel(block, rows_ref, count_ref, win_ref, wout_ref, w1_ref, w2_ref):
    chunk = pl.program_id(0)
    per, _, slots = win_ref.shape[:3]
    w1_ref[...] = jnp.zeros_like(w1_ref)
    w2_ref[...] = jnp.zeros_like(w2_ref)
    for j in range(per):
        column = chunk * per + j
        for s in range(slots):
            used = s < count_ref[column]
            at = pl.ds(pl.multiple_of(rows_ref[column * slots + s] * block, block), block)
            here = slice(j * block, (j + 1) * block)
            tile_in = win_ref[j, 0, s]
            tile_out = wout_ref[j, 0, s]
            w1_ref[0, at, here] = jnp.where(used, tile_in, jnp.zeros_like(tile_in))
            w2_ref[0, here, at] = jnp.where(used, tile_out, jnp.zeros_like(tile_out))


def expand(rows, counts, weight_in, weight_out, features, per):
    columns, _, slots, block, _ = weight_in.shape
    width = per * block
    chunks = columns // per
    tile_spec = pl.BlockSpec((per, 1, slots, block, block), lambda c, *_: (c, 0, 0, 0, 0))
    return pl.pallas_call(
        functools.partial(expand_kernel, block),
        grid_spec=pltpu.PrefetchScalarGridSpec(
            num_scalar_prefetch=2,
            grid=(chunks,),
            in_specs=[tile_spec, tile_spec],
            out_specs=[
                pl.BlockSpec((1, features, width), lambda c, *_: (c, 0, 0)),
                pl.BlockSpec((1, width, features), lambda c, *_: (c, 0, 0)),
            ],
        ),
        out_shape=[
            jax.ShapeDtypeStruct((chunks, features, width), jnp.bfloat16),
            jax.ShapeDtypeStruct((chunks, width, features), jnp.bfloat16),
        ],
        compiler_params=pltpu.CompilerParams(vmem_limit_bytes=VMEM_LIMIT),
        cost_estimate=pl.CostEstimate(
            flops=0, bytes_accessed=chunks * width * features * 5, transcendentals=0
        ),
        name="expand_tiles",
    )(rows, counts, weight_in, weight_out)


class Side:
    def __init__(self, ways, refs, tail):
        self.ways = ways
        if ways:
            (self.part, self.other, self.result, self.landed, self.sent, self.came) = refs
            self.half = self.result.shape[0]
            self.me = lax.axis_index("wide")
        self.tail = tail

    def rows(self, index):
        return pl.ds(pl.multiple_of(index * self.half, self.half), self.half)

    def peer(self, k):
        return lax.rem(self.me + k, self.ways)

    def part_copy(self, k):
        return pltpu.make_async_remote_copy(
            src_ref=self.part.at[self.rows(self.peer(k))],
            dst_ref=self.landed.at[k],
            send_sem=self.sent.at[k],
            recv_sem=self.came.at[k],
            device_id={"wide": self.peer(k)},
            device_id_type=MESH,
        )

    def error_copy(self, k):
        _, held, sent, came = self.tail
        return pltpu.make_async_remote_copy(
            src_ref=held.at[self.rows(self.me)],
            dst_ref=held.at[self.rows(self.me)],
            send_sem=sent.at[k],
            recv_sem=came.at[k],
            device_id={"wide": self.peer(k)},
            device_id_type=MESH,
        )

    def greet(self, barrier):
        for k in range(1, self.ways):
            pl.semaphore_signal(
                barrier, inc=1, device_id={"wide": self.peer(k)}, device_id_type=MESH
            )

    def start(self):
        for k in range(1, self.ways):
            self.part_copy(k).start()

    def middle(self):
        total = self.part[self.rows(self.me), :].astype(jnp.float32)
        for k in range(1, self.ways):
            self.part_copy(k).wait_recv()
            total = total + self.landed[k].astype(jnp.float32)
        if self.tail is None:
            self.result[...] = (total * self.other[0, 0]).astype(jnp.bfloat16)
            return
        mine = total.astype(jnp.bfloat16)
        self.result[...] = mine
        held = self.tail[1]
        held[self.rows(self.me), :] = (
            mine.astype(jnp.float32) - self.other[...].astype(jnp.float32)
        ).astype(jnp.bfloat16)
        for k in range(1, self.ways):
            self.error_copy(k).start()

    def end(self):
        for k in range(1, self.ways):
            self.part_copy(k).wait_send()
        if self.ways and self.tail is not None:
            for k in range(1, self.ways):
                self.error_copy(k).wait()
            self.tail[0][...] = self.tail[1][...]


def line_sum_loop(
    n, side, chunks, own_of, finish, own, to_right, to_left, from_left, from_right, sems, panels
):
    right_sent, left_sent, left_came, right_came = sems
    first_hbm, first_buf, first_sem, last_hbm, last_buf, last_sem = panels
    me = lax.axis_index("blk")
    right = jnp.minimum(me + 1, n - 1)
    left = jnp.maximum(me - 1, 0)

    def right_copy(c):
        return pltpu.make_async_remote_copy(
            src_ref=to_right.at[c],
            dst_ref=from_left.at[c],
            send_sem=right_sent.at[c],
            recv_sem=left_came.at[c],
            device_id={"blk": right},
            device_id_type=MESH,
        )

    def left_copy(c):
        return pltpu.make_async_remote_copy(
            src_ref=to_left.at[c],
            dst_ref=from_right.at[c],
            send_sem=left_sent.at[c],
            recv_sem=right_came.at[c],
            device_id={"blk": left},
            device_id_type=MESH,
        )

    def first_copy(c):
        slot = lax.rem(c, RING)
        return pltpu.make_async_copy(first_hbm.at[c], first_buf.at[slot], first_sem.at[slot])

    def last_copy(c):
        slot = lax.rem(c, RING)
        return pltpu.make_async_copy(last_hbm.at[c], last_buf.at[slot], last_sem.at[slot])

    for c in range(min(RING, chunks)):
        first_copy(jnp.int32(c)).start()
        last_copy(jnp.int32(c)).start()

    @pl.when(me == 0)
    def _():
        from_left[...] = jnp.zeros_like(from_left)

    @pl.when(me == n - 1)
    def _():
        from_right[...] = jnp.zeros_like(from_right)

    barrier = pltpu.get_barrier_semaphore()

    @pl.when(me > 0)
    def _():
        pl.semaphore_signal(barrier, inc=1, device_id={"blk": left}, device_id_type=MESH)

    @pl.when(me < n - 1)
    def _():
        pl.semaphore_signal(barrier, inc=1, device_id={"blk": right}, device_id_type=MESH)

    side.greet(barrier)
    peers = jnp.where(me > 0, 1, 0) + jnp.where(me < n - 1, 1, 0)
    pl.semaphore_wait(barrier, peers + max(side.ways - 1, 0))
    side.start()
    steps = chunks + LAG * (n - 1)

    def step(t, carry):
        if side.ways:
            pl.when(t == (2 * steps) // 5)(side.middle)

        @pl.when(t < chunks)
        def _():
            first_copy(t).wait()
            own[t] = own_of(first_buf[lax.rem(t, RING)])

            @pl.when(t + RING < chunks)
            def _():
                first_copy(t + RING).start()

        onward = t - LAG * me

        @pl.when((onward >= 0) & (onward < chunks))
        def _():
            @pl.when(me > 0)
            def _():
                right_copy(onward).wait_recv()

            @pl.when(me < n - 1)
            def _():
                to_right[onward] = (
                    own[onward] + from_left[onward].astype(jnp.float32)
                ).astype(jnp.bfloat16)
                right_copy(onward).start()

        back = t - LAG * (n - 1 - me)

        @pl.when((back >= 0) & (back < chunks))
        def _():
            @pl.when(me < n - 1)
            def _():
                left_copy(back).wait_recv()

            @pl.when(me > 0)
            def _():
                to_left[back] = (
                    own[back] + from_right[back].astype(jnp.float32)
                ).astype(jnp.bfloat16)
                left_copy(back).start()

        done = t - LAG * (n - 1)

        @pl.when(done >= 0)
        def _():
            last_copy(done).wait()
            total = (
                own[done]
                + from_left[done].astype(jnp.float32)
                + from_right[done].astype(jnp.float32)
            )
            finish(done, total, last_buf[lax.rem(done, RING)])

            @pl.when(done + RING < chunks)
            def _():
                last_copy(done + RING).start()

        return carry

    lax.fori_loop(0, steps, step, 0)
    side.end()

    def drain(c, carry):
        @pl.when(me < n - 1)
        def _():
            right_copy(c).wait_send()

        @pl.when(me > 0)
        def _():
            left_copy(c).wait_send()

        return carry

    lax.fori_loop(0, chunks, drain, 0)


NT = (((1,), (1,)), ((), ()))


def split_refs(ways, gathers, outs, refs):
    refs = list(refs)
    take = lambda count: [refs.pop(0) for _ in range(count)]
    side_in = take(2 if ways else 0)
    main_out = take(outs)
    side_out = take((2 if gathers else 1) if ways else 0)
    scratch = take(14)
    if not ways:
        return Side(0, None, None), main_out, scratch
    landed, sent, came = take(3)
    tail = (side_out[1], *take(3)) if gathers else None
    return Side(ways, (*side_in, side_out[0], landed, sent, came), tail), main_out, scratch


def side_specs(side):
    if side is None:
        return 0, False, (), [], [], []
    ways, gathers, part, other = side
    half, features = part.shape[0] // ways, part.shape[1]
    shapes = [jax.ShapeDtypeStruct((half, features), jnp.bfloat16)]
    sems = pltpu.SemaphoreType.DMA((ways,))
    scratch = [pltpu.VMEM((ways, half, features), jnp.bfloat16), sems, sems]
    if gathers:
        shapes.append(jax.ShapeDtypeStruct(part.shape, jnp.bfloat16))
        scratch += [pltpu.VMEM(part.shape, jnp.bfloat16), sems, sems]
    other_spec = VM if gathers else pl.BlockSpec(memory_space=pltpu.SMEM)
    return ways, gathers, (part, other), [VM, other_spec], shapes, scratch


def forward_kernel(
    n, ways, gathers, inv_ref, x_ref, w1_hbm, w2_hbm, *refs,
):
    side, (out_ref, hidden_ref, active_ref), scratch = split_refs(ways, gathers, 3, refs)
    acc, own, to_right, to_left, from_left, from_right, s0, s1, s2, s3, b1, m1, b2, m2 = scratch
    chunks = w1_hbm.shape[0]
    acc[...] = jnp.zeros_like(acc)

    def own_of(panel):
        return jnp.dot(x_ref[...], panel, preferred_element_type=jnp.float32)

    def finish(c, total, panel):
        value = total * inv_ref[0, 0]
        curve = jnp.tanh(RATE * (value + CUBIC * value * value * value))
        active = (0.5 * value * (1.0 + curve)).astype(jnp.bfloat16)
        hidden_ref[c] = value.astype(jnp.bfloat16)
        active_ref[c] = active
        acc[...] += jnp.dot(active, panel, preferred_element_type=jnp.float32)

    line_sum_loop(
        n, side, chunks, own_of, finish, own, to_right, to_left, from_left, from_right,
        (s0, s1, s2, s3), (w1_hbm, b1, m1, w2_hbm, b2, m2),
    )
    out_ref[...] = acc[...].astype(jnp.bfloat16)


def backward_kernel(
    n, ways, gathers, e_ref, hidden_ref, w2_hbm, w1_hbm, *refs,
):
    side, (out_ref, slope_ref, curv_ref), scratch = split_refs(ways, gathers, 3, refs)
    acc, own, to_right, to_left, from_left, from_right, s0, s1, s2, s3, b1, m1, b2, m2 = scratch
    chunks = w1_hbm.shape[0]
    acc[...] = jnp.zeros_like(acc)
    curv_ref[...] = jnp.zeros_like(curv_ref)

    def own_of(panel):
        return lax.dot_general(e_ref[...], panel, NT, preferred_element_type=jnp.float32)

    def finish(c, total, panel):
        value = hidden_ref[c].astype(jnp.float32)
        square = value * value
        curve = jnp.tanh(RATE * (value + CUBIC * value * square))
        rise = 0.5 * (1.0 + curve) + 0.5 * value * (1.0 - curve * curve) * (
            RATE * (1.0 + 3.0 * CUBIC * square)
        )
        wide_slope = total * rise
        slope = wide_slope.astype(jnp.bfloat16)
        slope_ref[c] = slope
        rows, cols = value.shape
        curv_ref[...] += jnp.sum((wide_slope * value).reshape(rows // 8, 8, cols), axis=0)
        acc[...] += lax.dot_general(slope, panel, NT, preferred_element_type=jnp.float32)

    line_sum_loop(
        n, side, chunks, own_of, finish, own, to_right, to_left, from_left, from_right,
        (s0, s1, s2, s3), (w2_hbm, b1, m1, w1_hbm, b2, m2),
    )
    out_ref[...] = acc[...].astype(jnp.bfloat16)


def scratch_for(chunks, rows, width, features, first, last):
    moved = pltpu.VMEM((chunks, rows, width), jnp.bfloat16)
    return [
        pltpu.VMEM((rows, features), jnp.float32),
        pltpu.VMEM((chunks, rows, width), jnp.float32),
        moved, moved, moved, moved,
        *[pltpu.SemaphoreType.DMA((chunks,)) for _ in range(4)],
        pltpu.VMEM((RING,) + first, jnp.bfloat16),
        pltpu.SemaphoreType.DMA((RING,)),
        pltpu.VMEM((RING,) + last, jnp.bfloat16),
        pltpu.SemaphoreType.DMA((RING,)),
    ]


def line_cost(chunks, rows, width, features):
    return pl.CostEstimate(
        flops=chunks * width * features * rows * 4 * 8,
        bytes_accessed=chunks * width * features * 4,
        transcendentals=chunks * rows * width,
    )


VM = pl.BlockSpec(memory_space=pltpu.VMEM)
ANY = pl.BlockSpec(memory_space=pl.ANY)


def forward_half(n, inv, x, w1, w2, ident, side=None):
    ways, gathers, more, more_specs, more_shapes, more_scratch = side_specs(side)
    chunks, features, width = w1.shape
    rows = x.shape[0]
    kept = jax.ShapeDtypeStruct((chunks, rows, width), jnp.bfloat16)
    return pl.pallas_call(
        functools.partial(forward_kernel, n, ways, gathers),
        out_shape=[jax.ShapeDtypeStruct((rows, features), jnp.bfloat16), kept, kept] + more_shapes,
        in_specs=[pl.BlockSpec(memory_space=pltpu.SMEM), VM, ANY, ANY] + more_specs,
        out_specs=[VM] * (3 + len(more_shapes)),
        scratch_shapes=scratch_for(
            chunks, rows, width, features, (features, width), (width, features)
        ) + more_scratch,
        compiler_params=pltpu.CompilerParams(
            collective_id=ident, has_side_effects=True, vmem_limit_bytes=VMEM_LIMIT
        ),
        cost_estimate=line_cost(chunks, rows, width, features),
        name="forward_half_" + "ab"[ident],
    )(inv, x, w1, w2, *more)


def backward_half(n, err, hidden, w2, w1, ident, side=None):
    ways, gathers, more, more_specs, more_shapes, more_scratch = side_specs(side)
    chunks, features, width = w1.shape
    rows = err.shape[0]
    return pl.pallas_call(
        functools.partial(backward_kernel, n, ways, gathers),
        out_shape=[
            jax.ShapeDtypeStruct((rows, features), jnp.bfloat16),
            jax.ShapeDtypeStruct((chunks, rows, width), jnp.bfloat16),
            jax.ShapeDtypeStruct((8, width), jnp.float32),
        ] + more_shapes,
        in_specs=[VM, VM, ANY, ANY] + more_specs,
        out_specs=[VM] * (3 + len(more_shapes)),
        scratch_shapes=scratch_for(
            chunks, rows, width, features, (width, features), (features, width)
        ) + more_scratch,
        compiler_params=pltpu.CompilerParams(
            collective_id=2 + ident, has_side_effects=True, vmem_limit_bytes=VMEM_LIMIT
        ),
        cost_estimate=line_cost(chunks, rows, width, features),
        name="backward_half_" + "ab"[ident],
    )(err, hidden, w2, w1, *more)


TN = (((0,), (0,)), ((), ()))


def tile_grad_kernel(block, picked_first, rows_ref, count_ref, fa_ref, fb_ref, ha_ref, hb_ref, out_ref):
    chunk = pl.program_id(0)
    per, _, slots = out_ref.shape[:3]
    for j in range(per):
        column = chunk * per + j
        here = slice(j * block, (j + 1) * block)
        hidden_a = ha_ref[0, :, here]
        hidden_b = hb_ref[0, :, here]
        for s in range(slots):
            used = s < count_ref[column]
            at = pl.ds(pl.multiple_of(rows_ref[column * slots + s] * block, block), block)
            pick_a = fa_ref[:, at]
            pick_b = fb_ref[:, at]
            pairs = ((pick_a, hidden_a), (pick_b, hidden_b))
            total = 0.0
            for pick, hid in pairs:
                ends = (pick, hid) if picked_first else (hid, pick)
                total = total + lax.dot_general(*ends, TN, preferred_element_type=jnp.float32)
            out_ref[j, 0, s] = jnp.where(used, total, jnp.zeros_like(total))


def tile_grad(rows, counts, feat_a, feat_b, hid_a, hid_b, shape, picked_first, name):
    columns, _, slots, block, _ = shape
    chunks, _, width = hid_a.shape
    per = width // block
    whole = pl.BlockSpec(feat_a.shape, lambda c, *_: (0, 0))
    part = pl.BlockSpec((1,) + hid_a.shape[1:], lambda c, *_: (c, 0, 0))
    return pl.pallas_call(
        functools.partial(tile_grad_kernel, block, picked_first),
        grid_spec=pltpu.PrefetchScalarGridSpec(
            num_scalar_prefetch=2,
            grid=(chunks,),
            in_specs=[whole, whole, part, part],
            out_specs=pl.BlockSpec((per, 1, slots, block, block), lambda c, *_: (c, 0, 0, 0, 0)),
        ),
        out_shape=jax.ShapeDtypeStruct(shape, jnp.float32),
        compiler_params=pltpu.CompilerParams(vmem_limit_bytes=VMEM_LIMIT),
        cost_estimate=pl.CostEstimate(
            flops=columns * slots * block * block * feat_a.shape[0] * 4 * 8,
            bytes_accessed=columns * slots * block * block * 12,
            transcendentals=0,
        ),
        name=name,
    )(rows, counts, feat_a, feat_b, hid_a, hid_b)


def body(n, ways, tokens, target, probe_vector, weight_in, weight_out, slot_rows, slot_count):
    columns, unit, slots, block, width_two = weight_in.shape
    owned, features = tokens.shape
    feature_blocks = features // block
    per = 2
    half = owned // 2
    row_index = slot_rows[:, 0]
    flat_rows = row_index.reshape(-1)
    flat_count = slot_count.reshape(-1)

    def gather(piece):
        return lax.all_gather(piece, "wide", axis=0, tiled=True)

    def scatter(piece):
        return lax.psum_scatter(piece, "wide", scatter_dimension=0, tiled=True)

    x_a = gather(tokens[:half])
    x_b = gather(tokens[half:])

    in_use = lax.broadcasted_iota(jnp.int32, (columns, slots), 1) < slot_count[:, 0][:, None]
    mask_low = in_use.astype(jnp.bfloat16)[:, :, None, None]
    mask_full = in_use.astype(jnp.float32)[:, :, None, None]
    tiles_in = weight_in[:, 0] * mask_low
    chosen = jnp.take(probe_vector.reshape(feature_blocks, block), flat_rows, axis=0).reshape(
        columns, slots, block
    )
    image_part = jnp.einsum(
        "jsk,jskn->jn", chosen, tiles_in.astype(jnp.float32), precision=lax.Precision.HIGHEST
    )
    image, norm_probe = lax.psum((image_part, jnp.sum(probe_vector * probe_vector)), "blk")
    norm_image = lax.psum(jnp.sum(image * image), "wide")
    spectral = jnp.sqrt(norm_image / norm_probe)
    inverse = (1.0 / spectral).reshape(1, 1)

    w1, w2 = expand(flat_rows, flat_count, weight_in, weight_out, features, per)

    part_a, hidden_a, active_a = forward_half(n, inverse, x_a, w1, w2, 0)
    part_b, hidden_b, active_b, out_a, err_a = forward_half(
        n, inverse, x_b, w1, w2, 1, (ways, True, part_a, target[:half])
    )
    back_a, slope_a, curv_a, out_b, err_b = backward_half(
        n, err_a, hidden_a, w2, w1, 0, (ways, True, part_b, target[half:])
    )
    back_b, slope_b, curv_b, grad_a = backward_half(
        n, err_b, hidden_b, w2, w1, 1, (ways, False, back_a, inverse)
    )
    grad_b = (scatter(back_b).astype(jnp.float32) / spectral).astype(jnp.bfloat16)
    curvature = spectral * lax.psum(jnp.sum(curv_a + curv_b), "wide")
    grad_out = tile_grad(
        flat_rows, flat_count, err_a, err_b, active_a, active_b, weight_out.shape, False, "grad_out"
    )
    raw_in = tile_grad(
        flat_rows, flat_count, x_a, x_b, slope_a, slope_b, weight_in.shape, True, "raw_in"
    )
    outer = jnp.einsum("jsk,jn->jskn", chosen, image) * mask_full
    grad_in = raw_in / spectral - (curvature / (spectral**3 * norm_probe) * outer)[:, None]
    outputs = jnp.concatenate([out_a, out_b], axis=0)
    token_grad = jnp.concatenate([grad_a, grad_b], axis=0)
    return (outputs, token_grad, grad_in, grad_out)


def solution(mesh):
    in_specs = (
        P("wide", "blk"),
        P("wide", "blk"),
        P("blk"),
        P("wide", "blk", None, None, None),
        P("wide", "blk", None, None, None),
        P("wide", "blk", None),
        P("wide", "blk"),
    )
    out_specs = (
        P("wide", "blk"),
        P("wide", "blk"),
        P("wide", "blk", None, None, None),
        P("wide", "blk", None, None, None),
    )
    return jax.shard_map(
        functools.partial(body, mesh.shape["blk"], mesh.shape["wide"]),
        mesh=mesh,
        in_specs=in_specs,
        out_specs=out_specs,
        check_vma=False,
    )
```

```python
import functools
import math

import jax
import jax.numpy as jnp
from jax import lax
from jax.experimental import pallas as pl
from jax.experimental.pallas import tpu as pltpu
from jax.sharding import PartitionSpec as P

MESH = pl.DeviceIdType.MESH
RATE = math.sqrt(2.0 / math.pi)
CUBIC = 0.044715
LAG = 2
RING = 3
VMEM_LIMIT = 48 * 1024 * 1024


def expand_kernel(block, rows_ref, count_ref, win_ref, wout_ref, w1_ref, w2_ref):
    chunk = pl.program_id(0)
    per, _, slots = win_ref.shape[:3]
    w1_ref[...] = jnp.zeros_like(w1_ref)
    w2_ref[...] = jnp.zeros_like(w2_ref)
    for j in range(per):
        column = chunk * per + j
        for s in range(slots):
            used = s < count_ref[column]
            at = pl.ds(pl.multiple_of(rows_ref[column * slots + s] * block, block), block)
            here = slice(j * block, (j + 1) * block)
            tile_in = win_ref[j, 0, s]
            tile_out = wout_ref[j, 0, s]
            w1_ref[0, at, here] = jnp.where(used, tile_in, jnp.zeros_like(tile_in))
            w2_ref[0, here, at] = jnp.where(used, tile_out, jnp.zeros_like(tile_out))


def expand(rows, counts, weight_in, weight_out, features, per):
    columns, _, slots, block, _ = weight_in.shape
    width = per * block
    chunks = columns // per
    tile_spec = pl.BlockSpec((per, 1, slots, block, block), lambda c, *_: (c, 0, 0, 0, 0))
    return pl.pallas_call(
        functools.partial(expand_kernel, block),
        grid_spec=pltpu.PrefetchScalarGridSpec(
            num_scalar_prefetch=2,
            grid=(chunks,),
            in_specs=[tile_spec, tile_spec],
            out_specs=[
                pl.BlockSpec((1, features, width), lambda c, *_: (c, 0, 0)),
                pl.BlockSpec((1, width, features), lambda c, *_: (c, 0, 0)),
            ],
        ),
        out_shape=[
            jax.ShapeDtypeStruct((chunks, features, width), jnp.bfloat16),
            jax.ShapeDtypeStruct((chunks, width, features), jnp.bfloat16),
        ],
        compiler_params=pltpu.CompilerParams(vmem_limit_bytes=VMEM_LIMIT),
        cost_estimate=pl.CostEstimate(
            flops=0, bytes_accessed=chunks * width * features * 5, transcendentals=0
        ),
        name="expand_tiles",
    )(rows, counts, weight_in, weight_out)


class Side:
    def __init__(self, ways, refs, tail):
        self.ways = ways
        if ways:
            (self.part, self.other, self.result, self.landed, self.sent, self.came) = refs
            self.half = self.result.shape[0]
            self.me = lax.axis_index("wide")
        self.tail = tail

    def rows(self, index):
        return pl.ds(pl.multiple_of(index * self.half, self.half), self.half)

    def peer(self, k):
        return lax.rem(self.me + k, self.ways)

    def part_copy(self, k):
        return pltpu.make_async_remote_copy(
            src_ref=self.part.at[self.rows(self.peer(k))],
            dst_ref=self.landed.at[k],
            send_sem=self.sent.at[k],
            recv_sem=self.came.at[k],
            device_id={"wide": self.peer(k)},
            device_id_type=MESH,
        )

    def error_copy(self, k):
        _, held, sent, came = self.tail
        return pltpu.make_async_remote_copy(
            src_ref=held.at[self.rows(self.me)],
            dst_ref=held.at[self.rows(self.me)],
            send_sem=sent.at[k],
            recv_sem=came.at[k],
            device_id={"wide": self.peer(k)},
            device_id_type=MESH,
        )

    def greet(self, barrier):
        for k in range(1, self.ways):
            pl.semaphore_signal(
                barrier, inc=1, device_id={"wide": self.peer(k)}, device_id_type=MESH
            )

    def start(self):
        for k in range(1, self.ways):
            self.part_copy(k).start()

    def middle(self):
        total = self.part[self.rows(self.me), :].astype(jnp.float32)
        for k in range(1, self.ways):
            self.part_copy(k).wait_recv()
            total = total + self.landed[k].astype(jnp.float32)
        if self.tail is None:
            self.result[...] = (total * self.other[0, 0]).astype(jnp.bfloat16)
            return
        mine = total.astype(jnp.bfloat16)
        self.result[...] = mine
        held = self.tail[1]
        held[self.rows(self.me), :] = (
            mine.astype(jnp.float32) - self.other[...].astype(jnp.float32)
        ).astype(jnp.bfloat16)
        for k in range(1, self.ways):
            self.error_copy(k).start()

    def end(self):
        for k in range(1, self.ways):
            self.part_copy(k).wait_send()
        if self.ways and self.tail is not None:
            for k in range(1, self.ways):
                self.error_copy(k).wait()
            self.tail[0][...] = self.tail[1][...]


def line_sum_loop(
    n, side, chunks, own_of, finish, own, to_right, to_left, from_left, from_right, sems, panels
):
    right_sent, left_sent, left_came, right_came = sems
    first_hbm, first_buf, first_sem, last_hbm, last_buf, last_sem = panels
    me = lax.axis_index("blk")
    right = jnp.minimum(me + 1, n - 1)
    left = jnp.maximum(me - 1, 0)

    def right_copy(c):
        return pltpu.make_async_remote_copy(
            src_ref=to_right.at[c],
            dst_ref=from_left.at[c],
            send_sem=right_sent.at[c],
            recv_sem=left_came.at[c],
            device_id={"blk": right},
            device_id_type=MESH,
        )

    def left_copy(c):
        return pltpu.make_async_remote_copy(
            src_ref=to_left.at[c],
            dst_ref=from_right.at[c],
            send_sem=left_sent.at[c],
            recv_sem=right_came.at[c],
            device_id={"blk": left},
            device_id_type=MESH,
        )

    def first_copy(c):
        slot = lax.rem(c, RING)
        return pltpu.make_async_copy(first_hbm.at[c], first_buf.at[slot], first_sem.at[slot])

    def last_copy(c):
        slot = lax.rem(c, RING)
        return pltpu.make_async_copy(last_hbm.at[c], last_buf.at[slot], last_sem.at[slot])

    for c in range(min(RING, chunks)):
        first_copy(jnp.int32(c)).start()
        last_copy(jnp.int32(c)).start()

    @pl.when(me == 0)
    def _():
        from_left[...] = jnp.zeros_like(from_left)

    @pl.when(me == n - 1)
    def _():
        from_right[...] = jnp.zeros_like(from_right)

    barrier = pltpu.get_barrier_semaphore()

    @pl.when(me > 0)
    def _():
        pl.semaphore_signal(barrier, inc=1, device_id={"blk": left}, device_id_type=MESH)

    @pl.when(me < n - 1)
    def _():
        pl.semaphore_signal(barrier, inc=1, device_id={"blk": right}, device_id_type=MESH)

    side.greet(barrier)
    peers = jnp.where(me > 0, 1, 0) + jnp.where(me < n - 1, 1, 0)
    pl.semaphore_wait(barrier, peers + max(side.ways - 1, 0))
    side.start()
    steps = chunks + LAG * (n - 1)

    def step(t, carry):
        if side.ways:
            pl.when(t == (2 * steps) // 5)(side.middle)

        @pl.when(t < chunks)
        def _():
            first_copy(t).wait()
            own[t] = own_of(first_buf[lax.rem(t, RING)])

            @pl.when(t + RING < chunks)
            def _():
                first_copy(t + RING).start()

        onward = t - LAG * me

        @pl.when((onward >= 0) & (onward < chunks))
        def _():
            @pl.when(me > 0)
            def _():
                right_copy(onward).wait_recv()

            @pl.when(me < n - 1)
            def _():
                to_right[onward] = (
                    own[onward] + from_left[onward].astype(jnp.float32)
                ).astype(jnp.bfloat16)
                right_copy(onward).start()

        back = t - LAG * (n - 1 - me)

        @pl.when((back >= 0) & (back < chunks))
        def _():
            @pl.when(me < n - 1)
            def _():
                left_copy(back).wait_recv()

            @pl.when(me > 0)
            def _():
                to_left[back] = (
                    own[back] + from_right[back].astype(jnp.float32)
                ).astype(jnp.bfloat16)
                left_copy(back).start()

        done = t - LAG * (n - 1)

        @pl.when(done >= 0)
        def _():
            last_copy(done).wait()
            total = (
                own[done]
                + from_left[done].astype(jnp.float32)
                + from_right[done].astype(jnp.float32)
            )
            finish(done, total, last_buf[lax.rem(done, RING)])

            @pl.when(done + RING < chunks)
            def _():
                last_copy(done + RING).start()

        return carry

    lax.fori_loop(0, steps, step, 0)
    side.end()

    def drain(c, carry):
        @pl.when(me < n - 1)
        def _():
            right_copy(c).wait_send()

        @pl.when(me > 0)
        def _():
            left_copy(c).wait_send()

        return carry

    lax.fori_loop(0, chunks, drain, 0)


NT = (((1,), (1,)), ((), ()))


def split_refs(ways, gathers, outs, refs):
    refs = list(refs)
    take = lambda count: [refs.pop(0) for _ in range(count)]
    side_in = take(2 if ways else 0)
    main_out = take(outs)
    side_out = take((2 if gathers else 1) if ways else 0)
    scratch = take(14)
    if not ways:
        return Side(0, None, None), main_out, scratch
    landed, sent, came = take(3)
    tail = (side_out[1], *take(3)) if gathers else None
    return Side(ways, (*side_in, side_out[0], landed, sent, came), tail), main_out, scratch


def side_specs(side):
    if side is None:
        return 0, False, (), [], [], []
    ways, gathers, part, other = side
    half, features = part.shape[0] // ways, part.shape[1]
    shapes = [jax.ShapeDtypeStruct((half, features), jnp.bfloat16)]
    sems = pltpu.SemaphoreType.DMA((ways,))
    scratch = [pltpu.VMEM((ways, half, features), jnp.bfloat16), sems, sems]
    if gathers:
        shapes.append(jax.ShapeDtypeStruct(part.shape, jnp.bfloat16))
        scratch += [pltpu.VMEM(part.shape, jnp.bfloat16), sems, sems]
    other_spec = VM if gathers else pl.BlockSpec(memory_space=pltpu.SMEM)
    return ways, gathers, (part, other), [VM, other_spec], shapes, scratch


def forward_kernel(
    n, ways, gathers, inv_ref, x_ref, w1_hbm, w2_hbm, *refs,
):
    side, (out_ref, hidden_ref, active_ref), scratch = split_refs(ways, gathers, 3, refs)
    acc, own, to_right, to_left, from_left, from_right, s0, s1, s2, s3, b1, m1, b2, m2 = scratch
    chunks = w1_hbm.shape[0]
    acc[...] = jnp.zeros_like(acc)

    def own_of(panel):
        return jnp.dot(x_ref[...], panel, preferred_element_type=jnp.float32)

    def finish(c, total, panel):
        value = total * inv_ref[0, 0]
        curve = jnp.tanh(RATE * (value + CUBIC * value * value * value))
        active = (0.5 * value * (1.0 + curve)).astype(jnp.bfloat16)
        hidden_ref[c] = value.astype(jnp.bfloat16)
        active_ref[c] = active
        acc[...] += jnp.dot(active, panel, preferred_element_type=jnp.float32)

    line_sum_loop(
        n, side, chunks, own_of, finish, own, to_right, to_left, from_left, from_right,
        (s0, s1, s2, s3), (w1_hbm, b1, m1, w2_hbm, b2, m2),
    )
    out_ref[...] = acc[...].astype(jnp.bfloat16)


def backward_kernel(
    n, ways, gathers, e_ref, hidden_ref, w2_hbm, w1_hbm, *refs,
):
    side, (out_ref, slope_ref, curv_ref), scratch = split_refs(ways, gathers, 3, refs)
    acc, own, to_right, to_left, from_left, from_right, s0, s1, s2, s3, b1, m1, b2, m2 = scratch
    chunks = w1_hbm.shape[0]
    acc[...] = jnp.zeros_like(acc)
    curv_ref[...] = jnp.zeros_like(curv_ref)

    def own_of(panel):
        return lax.dot_general(e_ref[...], panel, NT, preferred_element_type=jnp.float32)

    def finish(c, total, panel):
        value = hidden_ref[c].astype(jnp.float32)
        square = value * value
        curve = jnp.tanh(RATE * (value + CUBIC * value * square))
        rise = 0.5 * (1.0 + curve) + 0.5 * value * (1.0 - curve * curve) * (
            RATE * (1.0 + 3.0 * CUBIC * square)
        )
        wide_slope = total * rise
        slope = wide_slope.astype(jnp.bfloat16)
        slope_ref[c] = slope
        rows, cols = value.shape
        curv_ref[...] += jnp.sum((wide_slope * value).reshape(rows // 8, 8, cols), axis=0)
        acc[...] += lax.dot_general(slope, panel, NT, preferred_element_type=jnp.float32)

    line_sum_loop(
        n, side, chunks, own_of, finish, own, to_right, to_left, from_left, from_right,
        (s0, s1, s2, s3), (w2_hbm, b1, m1, w1_hbm, b2, m2),
    )
    out_ref[...] = acc[...].astype(jnp.bfloat16)


def scratch_for(chunks, rows, width, features, first, last):
    moved = pltpu.VMEM((chunks, rows, width), jnp.bfloat16)
    return [
        pltpu.VMEM((rows, features), jnp.float32),
        pltpu.VMEM((chunks, rows, width), jnp.float32),
        moved, moved, moved, moved,
        *[pltpu.SemaphoreType.DMA((chunks,)) for _ in range(4)],
        pltpu.VMEM((RING,) + first, jnp.bfloat16),
        pltpu.SemaphoreType.DMA((RING,)),
        pltpu.VMEM((RING,) + last, jnp.bfloat16),
        pltpu.SemaphoreType.DMA((RING,)),
    ]


def line_cost(chunks, rows, width, features):
    return pl.CostEstimate(
        flops=chunks * width * features * rows * 4 * 8,
        bytes_accessed=chunks * width * features * 4,
        transcendentals=chunks * rows * width,
    )


VM = pl.BlockSpec(memory_space=pltpu.VMEM)
ANY = pl.BlockSpec(memory_space=pl.ANY)


def forward_half(n, inv, x, w1, w2, ident, side=None):
    ways, gathers, more, more_specs, more_shapes, more_scratch = side_specs(side)
    chunks, features, width = w1.shape
    rows = x.shape[0]
    kept = jax.ShapeDtypeStruct((chunks, rows, width), jnp.bfloat16)
    return pl.pallas_call(
        functools.partial(forward_kernel, n, ways, gathers),
        out_shape=[jax.ShapeDtypeStruct((rows, features), jnp.bfloat16), kept, kept] + more_shapes,
        in_specs=[pl.BlockSpec(memory_space=pltpu.SMEM), VM, ANY, ANY] + more_specs,
        out_specs=[VM] * (3 + len(more_shapes)),
        scratch_shapes=scratch_for(
            chunks, rows, width, features, (features, width), (width, features)
        ) + more_scratch,
        compiler_params=pltpu.CompilerParams(
            collective_id=ident, has_side_effects=True, vmem_limit_bytes=VMEM_LIMIT
        ),
        cost_estimate=line_cost(chunks, rows, width, features),
        name="forward_half_" + "ab"[ident],
    )(inv, x, w1, w2, *more)


def backward_half(n, err, hidden, w2, w1, ident, side=None):
    ways, gathers, more, more_specs, more_shapes, more_scratch = side_specs(side)
    chunks, features, width = w1.shape
    rows = err.shape[0]
    return pl.pallas_call(
        functools.partial(backward_kernel, n, ways, gathers),
        out_shape=[
            jax.ShapeDtypeStruct((rows, features), jnp.bfloat16),
            jax.ShapeDtypeStruct((chunks, rows, width), jnp.bfloat16),
            jax.ShapeDtypeStruct((8, width), jnp.float32),
        ] + more_shapes,
        in_specs=[VM, VM, ANY, ANY] + more_specs,
        out_specs=[VM] * (3 + len(more_shapes)),
        scratch_shapes=scratch_for(
            chunks, rows, width, features, (width, features), (features, width)
        ) + more_scratch,
        compiler_params=pltpu.CompilerParams(
            collective_id=2 + ident, has_side_effects=True, vmem_limit_bytes=VMEM_LIMIT
        ),
        cost_estimate=line_cost(chunks, rows, width, features),
        name="backward_half_" + "ab"[ident],
    )(err, hidden, w2, w1, *more)


TN = (((0,), (0,)), ((), ()))


def tile_grad_kernel(block, picked_first, rows_ref, count_ref, fa_ref, fb_ref, ha_ref, hb_ref, out_ref):
    chunk = pl.program_id(0)
    per, _, slots = out_ref.shape[:3]
    for j in range(per):
        column = chunk * per + j
        here = slice(j * block, (j + 1) * block)
        hidden_a = ha_ref[0, :, here]
        hidden_b = hb_ref[0, :, here]
        for s in range(slots):
            used = s < count_ref[column]
            at = pl.ds(pl.multiple_of(rows_ref[column * slots + s] * block, block), block)
            pick_a = fa_ref[:, at]
            pick_b = fb_ref[:, at]
            pairs = ((pick_a, hidden_a), (pick_b, hidden_b))
            total = 0.0
            for pick, hid in pairs:
                ends = (pick, hid) if picked_first else (hid, pick)
                total = total + lax.dot_general(*ends, TN, preferred_element_type=jnp.float32)
            out_ref[j, 0, s] = jnp.where(used, total, jnp.zeros_like(total))


def tile_grad(rows, counts, feat_a, feat_b, hid_a, hid_b, shape, picked_first, name):
    columns, _, slots, block, _ = shape
    chunks, _, width = hid_a.shape
    per = width // block
    whole = pl.BlockSpec(feat_a.shape, lambda c, *_: (0, 0))
    part = pl.BlockSpec((1,) + hid_a.shape[1:], lambda c, *_: (c, 0, 0))
    return pl.pallas_call(
        functools.partial(tile_grad_kernel, block, picked_first),
        grid_spec=pltpu.PrefetchScalarGridSpec(
            num_scalar_prefetch=2,
            grid=(chunks,),
            in_specs=[whole, whole, part, part],
            out_specs=pl.BlockSpec((per, 1, slots, block, block), lambda c, *_: (c, 0, 0, 0, 0)),
        ),
        out_shape=jax.ShapeDtypeStruct(shape, jnp.float32),
        compiler_params=pltpu.CompilerParams(vmem_limit_bytes=VMEM_LIMIT),
        cost_estimate=pl.CostEstimate(
            flops=columns * slots * block * block * feat_a.shape[0] * 4 * 8,
            bytes_accessed=columns * slots * block * block * 12,
            transcendentals=0,
        ),
        name=name,
    )(rows, counts, feat_a, feat_b, hid_a, hid_b)


def small_sum_kernel(axis, size, value_ref, out_ref, landed, sent, came):
    me = lax.axis_index(axis)

    def copy(k):
        return pltpu.make_async_remote_copy(
            src_ref=value_ref,
            dst_ref=landed.at[me],
            send_sem=sent.at[k],
            recv_sem=came.at[k],
            device_id={axis: lax.rem(me + k, size)},
            device_id_type=MESH,
        )

    barrier = pltpu.get_barrier_semaphore()
    for k in range(1, size):
        pl.semaphore_signal(
            barrier, inc=1, device_id={axis: lax.rem(me + k, size)}, device_id_type=MESH
        )
    landed[me] = value_ref[...]
    pl.semaphore_wait(barrier, size - 1)
    for k in range(1, size):
        copy(k).start()
    for k in range(1, size):
        copy(k).wait()
    total = landed[0]
    for k in range(1, size):
        total = total + landed[k]
    out_ref[...] = total


def small_sum(value, axis, size, ident):
    sems = pltpu.SemaphoreType.DMA((size,))
    return pl.pallas_call(
        functools.partial(small_sum_kernel, axis, size),
        out_shape=jax.ShapeDtypeStruct(value.shape, jnp.float32),
        in_specs=[VM],
        out_specs=VM,
        scratch_shapes=[pltpu.VMEM((size,) + value.shape, jnp.float32), sems, sems],
        compiler_params=pltpu.CompilerParams(collective_id=ident, has_side_effects=True),
        cost_estimate=pl.CostEstimate(flops=1000, bytes_accessed=20000, transcendentals=0),
        name="small_sum_" + axis + "_" + str(ident),
    )(value)


def sum_wide(value, ways, ident):
    return small_sum(jnp.full((8, 128), value, jnp.float32), "wide", ways, ident)[0, 0]


def body(n, ways, tokens, target, probe_vector, weight_in, weight_out, slot_rows, slot_count):
    columns, unit, slots, block, width_two = weight_in.shape
    owned, features = tokens.shape
    feature_blocks = features // block
    per = 2
    half = owned // 2
    row_index = slot_rows[:, 0]
    flat_rows = row_index.reshape(-1)
    flat_count = slot_count.reshape(-1)

    def gather(piece):
        return lax.all_gather(piece, "wide", axis=0, tiled=True)

    def scatter(piece):
        return lax.psum_scatter(piece, "wide", scatter_dimension=0, tiled=True)

    x_a = gather(tokens[:half])
    x_b = gather(tokens[half:])

    in_use = lax.broadcasted_iota(jnp.int32, (columns, slots), 1) < slot_count[:, 0][:, None]
    mask_low = in_use.astype(jnp.bfloat16)[:, :, None, None]
    mask_full = in_use.astype(jnp.float32)[:, :, None, None]
    tiles_in = weight_in[:, 0] * mask_low
    chosen = jnp.take(probe_vector.reshape(feature_blocks, block), flat_rows, axis=0).reshape(
        columns, slots, block
    )
    image_part = jnp.einsum(
        "jsk,jskn->jn", chosen, tiles_in.astype(jnp.float32), precision=lax.Precision.HIGHEST
    )
    norm_part = jnp.full((8, block), jnp.sum(probe_vector * probe_vector), jnp.float32)
    summed = small_sum(jnp.concatenate([image_part, norm_part], axis=0), "blk", n, 4)
    image, norm_probe = summed[:columns], summed[columns, 0]
    norm_image = sum_wide(jnp.sum(image * image), ways, 5)
    spectral = jnp.sqrt(norm_image / norm_probe)
    inverse = (1.0 / spectral).reshape(1, 1)

    w1, w2 = expand(flat_rows, flat_count, weight_in, weight_out, features, per)

    part_a, hidden_a, active_a = forward_half(n, inverse, x_a, w1, w2, 0)
    part_b, hidden_b, active_b, out_a, err_a = forward_half(
        n, inverse, x_b, w1, w2, 1, (ways, True, part_a, target[:half])
    )
    back_a, slope_a, curv_a, out_b, err_b = backward_half(
        n, err_a, hidden_a, w2, w1, 0, (ways, True, part_b, target[half:])
    )
    back_b, slope_b, curv_b, grad_a = backward_half(
        n, err_b, hidden_b, w2, w1, 1, (ways, False, back_a, inverse)
    )
    grad_b = (scatter(back_b).astype(jnp.float32) / spectral).astype(jnp.bfloat16)
    curvature = spectral * sum_wide(jnp.sum(curv_a + curv_b), ways, 6)
    grad_out = tile_grad(
        flat_rows, flat_count, err_a, err_b, active_a, active_b, weight_out.shape, False, "grad_out"
    )
    raw_in = tile_grad(
        flat_rows, flat_count, x_a, x_b, slope_a, slope_b, weight_in.shape, True, "raw_in"
    )
    outer = jnp.einsum("jsk,jn->jskn", chosen, image) * mask_full
    grad_in = raw_in / spectral - (curvature / (spectral**3 * norm_probe) * outer)[:, None]
    outputs = jnp.concatenate([out_a, out_b], axis=0)
    token_grad = jnp.concatenate([grad_a, grad_b], axis=0)
    return (outputs, token_grad, grad_in, grad_out)


def solution(mesh):
    in_specs = (
        P("wide", "blk"),
        P("wide", "blk"),
        P("blk"),
        P("wide", "blk", None, None, None),
        P("wide", "blk", None, None, None),
        P("wide", "blk", None),
        P("wide", "blk"),
    )
    out_specs = (
        P("wide", "blk"),
        P("wide", "blk"),
        P("wide", "blk", None, None, None),
        P("wide", "blk", None, None, None),
    )
    return jax.shard_map(
        functools.partial(body, mesh.shape["blk"], mesh.shape["wide"]),
        mesh=mesh,
        in_specs=in_specs,
        out_specs=out_specs,
        check_vma=False,
    )
```

```python
import functools
import math

import jax
import jax.numpy as jnp
from jax import lax
from jax.experimental import pallas as pl
from jax.experimental.pallas import tpu as pltpu
from jax.sharding import PartitionSpec as P

MESH = pl.DeviceIdType.MESH
RATE = math.sqrt(2.0 / math.pi)
CUBIC = 0.044715
LAG = 1
RING = 3
VMEM_LIMIT = 48 * 1024 * 1024


def expand_kernel(block, rows_ref, count_ref, win_ref, wout_ref, w1_ref, w2_ref):
    chunk = pl.program_id(0)
    per, _, slots = win_ref.shape[:3]
    w1_ref[...] = jnp.zeros_like(w1_ref)
    w2_ref[...] = jnp.zeros_like(w2_ref)
    for j in range(per):
        column = chunk * per + j
        for s in range(slots):
            used = s < count_ref[column]
            at = pl.ds(pl.multiple_of(rows_ref[column * slots + s] * block, block), block)
            here = slice(j * block, (j + 1) * block)
            tile_in = win_ref[j, 0, s]
            tile_out = wout_ref[j, 0, s]
            w1_ref[0, at, here] = jnp.where(used, tile_in, jnp.zeros_like(tile_in))
            w2_ref[0, here, at] = jnp.where(used, tile_out, jnp.zeros_like(tile_out))


def expand(rows, counts, weight_in, weight_out, features, per):
    columns, _, slots, block, _ = weight_in.shape
    width = per * block
    chunks = columns // per
    tile_spec = pl.BlockSpec((per, 1, slots, block, block), lambda c, *_: (c, 0, 0, 0, 0))
    return pl.pallas_call(
        functools.partial(expand_kernel, block),
        grid_spec=pltpu.PrefetchScalarGridSpec(
            num_scalar_prefetch=2,
            grid=(chunks,),
            in_specs=[tile_spec, tile_spec],
            out_specs=[
                pl.BlockSpec((1, features, width), lambda c, *_: (c, 0, 0)),
                pl.BlockSpec((1, width, features), lambda c, *_: (c, 0, 0)),
            ],
        ),
        out_shape=[
            jax.ShapeDtypeStruct((chunks, features, width), jnp.bfloat16),
            jax.ShapeDtypeStruct((chunks, width, features), jnp.bfloat16),
        ],
        compiler_params=pltpu.CompilerParams(vmem_limit_bytes=VMEM_LIMIT),
        cost_estimate=pl.CostEstimate(
            flops=0, bytes_accessed=chunks * width * features * 5, transcendentals=0
        ),
        name="expand_tiles",
    )(rows, counts, weight_in, weight_out)


class Side:
    def __init__(self, ways, refs, tail):
        self.ways = ways
        if ways:
            (self.part, self.other, self.result, self.landed, self.sent, self.came) = refs
            self.half = self.result.shape[0]
            self.me = lax.axis_index("wide")
        self.tail = tail

    def rows(self, index):
        return pl.ds(pl.multiple_of(index * self.half, self.half), self.half)

    def peer(self, k):
        return lax.rem(self.me + k, self.ways)

    def part_copy(self, k):
        return pltpu.make_async_remote_copy(
            src_ref=self.part.at[self.rows(self.peer(k))],
            dst_ref=self.landed.at[k],
            send_sem=self.sent.at[k],
            recv_sem=self.came.at[k],
            device_id={"wide": self.peer(k)},
            device_id_type=MESH,
        )

    def error_copy(self, k):
        _, held, sent, came = self.tail
        return pltpu.make_async_remote_copy(
            src_ref=held.at[self.rows(self.me)],
            dst_ref=held.at[self.rows(self.me)],
            send_sem=sent.at[k],
            recv_sem=came.at[k],
            device_id={"wide": self.peer(k)},
            device_id_type=MESH,
        )

    def greet(self, barrier):
        for k in range(1, self.ways):
            pl.semaphore_signal(
                barrier, inc=1, device_id={"wide": self.peer(k)}, device_id_type=MESH
            )

    def start(self):
        for k in range(1, self.ways):
            self.part_copy(k).start()

    def middle(self):
        total = self.part[self.rows(self.me), :].astype(jnp.float32)
        for k in range(1, self.ways):
            self.part_copy(k).wait_recv()
            total = total + self.landed[k].astype(jnp.float32)
        if self.tail is None:
            self.result[...] = (total * self.other[0, 0]).astype(jnp.bfloat16)
            return
        mine = total.astype(jnp.bfloat16)
        self.result[...] = mine
        held = self.tail[1]
        held[self.rows(self.me), :] = (
            mine.astype(jnp.float32) - self.other[...].astype(jnp.float32)
        ).astype(jnp.bfloat16)
        for k in range(1, self.ways):
            self.error_copy(k).start()

    def end(self):
        for k in range(1, self.ways):
            self.part_copy(k).wait_send()
        if self.ways and self.tail is not None:
            for k in range(1, self.ways):
                self.error_copy(k).wait()
            self.tail[0][...] = self.tail[1][...]


def line_sum_loop(
    n, side, chunks, own_of, finish, own, to_right, to_left, from_left, from_right, sems, panels
):
    right_sent, left_sent, left_came, right_came = sems
    first_hbm, first_buf, first_sem, last_hbm, last_buf, last_sem = panels
    me = lax.axis_index("blk")
    right = jnp.minimum(me + 1, n - 1)
    left = jnp.maximum(me - 1, 0)

    def right_copy(c):
        return pltpu.make_async_remote_copy(
            src_ref=to_right.at[c],
            dst_ref=from_left.at[c],
            send_sem=right_sent.at[c],
            recv_sem=left_came.at[c],
            device_id={"blk": right},
            device_id_type=MESH,
        )

    def left_copy(c):
        return pltpu.make_async_remote_copy(
            src_ref=to_left.at[c],
            dst_ref=from_right.at[c],
            send_sem=left_sent.at[c],
            recv_sem=right_came.at[c],
            device_id={"blk": left},
            device_id_type=MESH,
        )

    def first_copy(c):
        slot = lax.rem(c, RING)
        return pltpu.make_async_copy(first_hbm.at[c], first_buf.at[slot], first_sem.at[slot])

    def last_copy(c):
        slot = lax.rem(c, RING)
        return pltpu.make_async_copy(last_hbm.at[c], last_buf.at[slot], last_sem.at[slot])

    for c in range(min(RING, chunks)):
        first_copy(jnp.int32(c)).start()
        last_copy(jnp.int32(c)).start()

    @pl.when(me == 0)
    def _():
        from_left[...] = jnp.zeros_like(from_left)

    @pl.when(me == n - 1)
    def _():
        from_right[...] = jnp.zeros_like(from_right)

    barrier = pltpu.get_barrier_semaphore()

    @pl.when(me > 0)
    def _():
        pl.semaphore_signal(barrier, inc=1, device_id={"blk": left}, device_id_type=MESH)

    @pl.when(me < n - 1)
    def _():
        pl.semaphore_signal(barrier, inc=1, device_id={"blk": right}, device_id_type=MESH)

    side.greet(barrier)
    peers = jnp.where(me > 0, 1, 0) + jnp.where(me < n - 1, 1, 0)
    pl.semaphore_wait(barrier, peers + max(side.ways - 1, 0))
    side.start()
    steps = chunks + LAG * (n - 1)

    def step(t, carry):
        if side.ways:
            pl.when(t == (2 * steps) // 5)(side.middle)

        @pl.when(t < chunks)
        def _():
            first_copy(t).wait()
            own[t] = own_of(first_buf[lax.rem(t, RING)])

            @pl.when(t + RING < chunks)
            def _():
                first_copy(t + RING).start()

        onward = t - LAG * me

        @pl.when((onward >= 0) & (onward < chunks))
        def _():
            @pl.when(me > 0)
            def _():
                right_copy(onward).wait_recv()

            @pl.when(me < n - 1)
            def _():
                to_right[onward] = (
                    own[onward] + from_left[onward].astype(jnp.float32)
                ).astype(jnp.bfloat16)
                right_copy(onward).start()

        back = t - LAG * (n - 1 - me)

        @pl.when((back >= 0) & (back < chunks))
        def _():
            @pl.when(me < n - 1)
            def _():
                left_copy(back).wait_recv()

            @pl.when(me > 0)
            def _():
                to_left[back] = (
                    own[back] + from_right[back].astype(jnp.float32)
                ).astype(jnp.bfloat16)
                left_copy(back).start()

        done = t - LAG * (n - 1)

        @pl.when(done >= 0)
        def _():
            last_copy(done).wait()
            total = (
                own[done]
                + from_left[done].astype(jnp.float32)
                + from_right[done].astype(jnp.float32)
            )
            finish(done, total, last_buf[lax.rem(done, RING)])

            @pl.when(done + RING < chunks)
            def _():
                last_copy(done + RING).start()

        return carry

    lax.fori_loop(0, steps, step, 0)
    side.end()

    def drain(c, carry):
        @pl.when(me < n - 1)
        def _():
            right_copy(c).wait_send()

        @pl.when(me > 0)
        def _():
            left_copy(c).wait_send()

        return carry

    lax.fori_loop(0, chunks, drain, 0)


NT = (((1,), (1,)), ((), ()))


def split_refs(ways, gathers, outs, refs):
    refs = list(refs)
    take = lambda count: [refs.pop(0) for _ in range(count)]
    side_in = take(2 if ways else 0)
    main_out = take(outs)
    side_out = take((2 if gathers else 1) if ways else 0)
    scratch = take(14)
    if not ways:
        return Side(0, None, None), main_out, scratch
    landed, sent, came = take(3)
    tail = (side_out[1], *take(3)) if gathers else None
    return Side(ways, (*side_in, side_out[0], landed, sent, came), tail), main_out, scratch


def side_specs(side):
    if side is None:
        return 0, False, (), [], [], []
    ways, gathers, part, other = side
    half, features = part.shape[0] // ways, part.shape[1]
    shapes = [jax.ShapeDtypeStruct((half, features), jnp.bfloat16)]
    sems = pltpu.SemaphoreType.DMA((ways,))
    scratch = [pltpu.VMEM((ways, half, features), jnp.bfloat16), sems, sems]
    if gathers:
        shapes.append(jax.ShapeDtypeStruct(part.shape, jnp.bfloat16))
        scratch += [pltpu.VMEM(part.shape, jnp.bfloat16), sems, sems]
    other_spec = VM if gathers else pl.BlockSpec(memory_space=pltpu.SMEM)
    return ways, gathers, (part, other), [VM, other_spec], shapes, scratch


def forward_kernel(
    n, ways, gathers, inv_ref, x_ref, w1_hbm, w2_hbm, *refs,
):
    side, (out_ref, hidden_ref, active_ref), scratch = split_refs(ways, gathers, 3, refs)
    acc, own, to_right, to_left, from_left, from_right, s0, s1, s2, s3, b1, m1, b2, m2 = scratch
    chunks = w1_hbm.shape[0]
    acc[...] = jnp.zeros_like(acc)

    def own_of(panel):
        return jnp.dot(x_ref[...], panel, preferred_element_type=jnp.float32)

    def finish(c, total, panel):
        value = total * inv_ref[0, 0]
        curve = jnp.tanh(RATE * (value + CUBIC * value * value * value))
        active = (0.5 * value * (1.0 + curve)).astype(jnp.bfloat16)
        hidden_ref[c] = value.astype(jnp.bfloat16)
        active_ref[c] = active
        acc[...] += jnp.dot(active, panel, preferred_element_type=jnp.float32)

    line_sum_loop(
        n, side, chunks, own_of, finish, own, to_right, to_left, from_left, from_right,
        (s0, s1, s2, s3), (w1_hbm, b1, m1, w2_hbm, b2, m2),
    )
    out_ref[...] = acc[...].astype(jnp.bfloat16)


def backward_kernel(
    n, ways, gathers, e_ref, hidden_ref, w2_hbm, w1_hbm, *refs,
):
    side, (out_ref, slope_ref, curv_ref), scratch = split_refs(ways, gathers, 3, refs)
    acc, own, to_right, to_left, from_left, from_right, s0, s1, s2, s3, b1, m1, b2, m2 = scratch
    chunks = w1_hbm.shape[0]
    acc[...] = jnp.zeros_like(acc)
    curv_ref[...] = jnp.zeros_like(curv_ref)

    def own_of(panel):
        return lax.dot_general(e_ref[...], panel, NT, preferred_element_type=jnp.float32)

    def finish(c, total, panel):
        value = hidden_ref[c].astype(jnp.float32)
        square = value * value
        curve = jnp.tanh(RATE * (value + CUBIC * value * square))
        rise = 0.5 * (1.0 + curve) + 0.5 * value * (1.0 - curve * curve) * (
            RATE * (1.0 + 3.0 * CUBIC * square)
        )
        wide_slope = total * rise
        slope = wide_slope.astype(jnp.bfloat16)
        slope_ref[c] = slope
        rows, cols = value.shape
        curv_ref[...] += jnp.sum((wide_slope * value).reshape(rows // 8, 8, cols), axis=0)
        acc[...] += lax.dot_general(slope, panel, NT, preferred_element_type=jnp.float32)

    line_sum_loop(
        n, side, chunks, own_of, finish, own, to_right, to_left, from_left, from_right,
        (s0, s1, s2, s3), (w2_hbm, b1, m1, w1_hbm, b2, m2),
    )
    out_ref[...] = acc[...].astype(jnp.bfloat16)


def scratch_for(chunks, rows, width, features, first, last):
    moved = pltpu.VMEM((chunks, rows, width), jnp.bfloat16)
    return [
        pltpu.VMEM((rows, features), jnp.float32),
        pltpu.VMEM((chunks, rows, width), jnp.float32),
        moved, moved, moved, moved,
        *[pltpu.SemaphoreType.DMA((chunks,)) for _ in range(4)],
        pltpu.VMEM((RING,) + first, jnp.bfloat16),
        pltpu.SemaphoreType.DMA((RING,)),
        pltpu.VMEM((RING,) + last, jnp.bfloat16),
        pltpu.SemaphoreType.DMA((RING,)),
    ]


def line_cost(chunks, rows, width, features):
    return pl.CostEstimate(
        flops=chunks * width * features * rows * 4 * 8,
        bytes_accessed=chunks * width * features * 4,
        transcendentals=chunks * rows * width,
    )


VM = pl.BlockSpec(memory_space=pltpu.VMEM)
ANY = pl.BlockSpec(memory_space=pl.ANY)


def forward_half(n, inv, x, w1, w2, ident, side=None):
    ways, gathers, more, more_specs, more_shapes, more_scratch = side_specs(side)
    chunks, features, width = w1.shape
    rows = x.shape[0]
    kept = jax.ShapeDtypeStruct((chunks, rows, width), jnp.bfloat16)
    return pl.pallas_call(
        functools.partial(forward_kernel, n, ways, gathers),
        out_shape=[jax.ShapeDtypeStruct((rows, features), jnp.bfloat16), kept, kept] + more_shapes,
        in_specs=[pl.BlockSpec(memory_space=pltpu.SMEM), VM, ANY, ANY] + more_specs,
        out_specs=[VM] * (3 + len(more_shapes)),
        scratch_shapes=scratch_for(
            chunks, rows, width, features, (features, width), (width, features)
        ) + more_scratch,
        compiler_params=pltpu.CompilerParams(
            collective_id=ident, has_side_effects=True, vmem_limit_bytes=VMEM_LIMIT
        ),
        cost_estimate=line_cost(chunks, rows, width, features),
        name="forward_half_" + "ab"[ident],
    )(inv, x, w1, w2, *more)


def backward_half(n, err, hidden, w2, w1, ident, side=None):
    ways, gathers, more, more_specs, more_shapes, more_scratch = side_specs(side)
    chunks, features, width = w1.shape
    rows = err.shape[0]
    return pl.pallas_call(
        functools.partial(backward_kernel, n, ways, gathers),
        out_shape=[
            jax.ShapeDtypeStruct((rows, features), jnp.bfloat16),
            jax.ShapeDtypeStruct((chunks, rows, width), jnp.bfloat16),
            jax.ShapeDtypeStruct((8, width), jnp.float32),
        ] + more_shapes,
        in_specs=[VM, VM, ANY, ANY] + more_specs,
        out_specs=[VM] * (3 + len(more_shapes)),
        scratch_shapes=scratch_for(
            chunks, rows, width, features, (width, features), (features, width)
        ) + more_scratch,
        compiler_params=pltpu.CompilerParams(
            collective_id=2 + ident, has_side_effects=True, vmem_limit_bytes=VMEM_LIMIT
        ),
        cost_estimate=line_cost(chunks, rows, width, features),
        name="backward_half_" + "ab"[ident],
    )(err, hidden, w2, w1, *more)


TN = (((0,), (0,)), ((), ()))


def tile_grad_kernel(block, picked_first, rows_ref, count_ref, fa_ref, fb_ref, ha_ref, hb_ref, out_ref):
    chunk = pl.program_id(0)
    per, _, slots = out_ref.shape[:3]
    for j in range(per):
        column = chunk * per + j
        here = slice(j * block, (j + 1) * block)
        hidden_a = ha_ref[0, :, here]
        hidden_b = hb_ref[0, :, here]
        for s in range(slots):
            used = s < count_ref[column]
            at = pl.ds(pl.multiple_of(rows_ref[column * slots + s] * block, block), block)
            pick_a = fa_ref[:, at]
            pick_b = fb_ref[:, at]
            pairs = ((pick_a, hidden_a), (pick_b, hidden_b))
            total = 0.0
            for pick, hid in pairs:
                ends = (pick, hid) if picked_first else (hid, pick)
                total = total + lax.dot_general(*ends, TN, preferred_element_type=jnp.float32)
            out_ref[j, 0, s] = jnp.where(used, total, jnp.zeros_like(total))


def tile_grad(rows, counts, feat_a, feat_b, hid_a, hid_b, shape, picked_first, name):
    columns, _, slots, block, _ = shape
    chunks, _, width = hid_a.shape
    per = width // block
    whole = pl.BlockSpec(feat_a.shape, lambda c, *_: (0, 0))
    part = pl.BlockSpec((1,) + hid_a.shape[1:], lambda c, *_: (c, 0, 0))
    return pl.pallas_call(
        functools.partial(tile_grad_kernel, block, picked_first),
        grid_spec=pltpu.PrefetchScalarGridSpec(
            num_scalar_prefetch=2,
            grid=(chunks,),
            in_specs=[whole, whole, part, part],
            out_specs=pl.BlockSpec((per, 1, slots, block, block), lambda c, *_: (c, 0, 0, 0, 0)),
        ),
        out_shape=jax.ShapeDtypeStruct(shape, jnp.float32),
        compiler_params=pltpu.CompilerParams(vmem_limit_bytes=VMEM_LIMIT),
        cost_estimate=pl.CostEstimate(
            flops=columns * slots * block * block * feat_a.shape[0] * 4 * 8,
            bytes_accessed=columns * slots * block * block * 12,
            transcendentals=0,
        ),
        name=name,
    )(rows, counts, feat_a, feat_b, hid_a, hid_b)


def small_sum_kernel(axis, size, value_ref, out_ref, landed, sent, came):
    me = lax.axis_index(axis)

    def copy(k):
        return pltpu.make_async_remote_copy(
            src_ref=value_ref,
            dst_ref=landed.at[me],
            send_sem=sent.at[k],
            recv_sem=came.at[k],
            device_id={axis: lax.rem(me + k, size)},
            device_id_type=MESH,
        )

    barrier = pltpu.get_barrier_semaphore()
    for k in range(1, size):
        pl.semaphore_signal(
            barrier, inc=1, device_id={axis: lax.rem(me + k, size)}, device_id_type=MESH
        )
    landed[me] = value_ref[...]
    pl.semaphore_wait(barrier, size - 1)
    for k in range(1, size):
        copy(k).start()
    for k in range(1, size):
        copy(k).wait()
    total = landed[0]
    for k in range(1, size):
        total = total + landed[k]
    out_ref[...] = total


def small_sum(value, axis, size, ident):
    sems = pltpu.SemaphoreType.DMA((size,))
    return pl.pallas_call(
        functools.partial(small_sum_kernel, axis, size),
        out_shape=jax.ShapeDtypeStruct(value.shape, jnp.float32),
        in_specs=[VM],
        out_specs=VM,
        scratch_shapes=[pltpu.VMEM((size,) + value.shape, jnp.float32), sems, sems],
        compiler_params=pltpu.CompilerParams(collective_id=ident, has_side_effects=True),
        cost_estimate=pl.CostEstimate(flops=1000, bytes_accessed=20000, transcendentals=0),
        name="small_sum_" + axis + "_" + str(ident),
    )(value)


def sum_wide(value, ways, ident):
    return small_sum(jnp.full((8, 128), value, jnp.float32), "wide", ways, ident)[0, 0]


def body(n, ways, tokens, target, probe_vector, weight_in, weight_out, slot_rows, slot_count):
    columns, unit, slots, block, width_two = weight_in.shape
    owned, features = tokens.shape
    feature_blocks = features // block
    per = 2
    half = owned // 2
    row_index = slot_rows[:, 0]
    flat_rows = row_index.reshape(-1)
    flat_count = slot_count.reshape(-1)

    def gather(piece):
        return lax.all_gather(piece, "wide", axis=0, tiled=True)

    def scatter(piece):
        return lax.psum_scatter(piece, "wide", scatter_dimension=0, tiled=True)

    x_a = gather(tokens[:half])
    x_b = gather(tokens[half:])

    in_use = lax.broadcasted_iota(jnp.int32, (columns, slots), 1) < slot_count[:, 0][:, None]
    mask_low = in_use.astype(jnp.bfloat16)[:, :, None, None]
    mask_full = in_use.astype(jnp.float32)[:, :, None, None]
    tiles_in = weight_in[:, 0] * mask_low
    chosen = jnp.take(probe_vector.reshape(feature_blocks, block), flat_rows, axis=0).reshape(
        columns, slots, block
    )
    image_part = jnp.einsum(
        "jsk,jskn->jn", chosen, tiles_in.astype(jnp.float32), precision=lax.Precision.HIGHEST
    )
    norm_part = jnp.full((8, block), jnp.sum(probe_vector * probe_vector), jnp.float32)
    summed = small_sum(jnp.concatenate([image_part, norm_part], axis=0), "blk", n, 4)
    image, norm_probe = summed[:columns], summed[columns, 0]
    norm_image = sum_wide(jnp.sum(image * image), ways, 5)
    spectral = jnp.sqrt(norm_image / norm_probe)
    inverse = (1.0 / spectral).reshape(1, 1)

    w1, w2 = expand(flat_rows, flat_count, weight_in, weight_out, features, per)

    part_a, hidden_a, active_a = forward_half(n, inverse, x_a, w1, w2, 0)
    part_b, hidden_b, active_b, out_a, err_a = forward_half(
        n, inverse, x_b, w1, w2, 1, (ways, True, part_a, target[:half])
    )
    back_a, slope_a, curv_a, out_b, err_b = backward_half(
        n, err_a, hidden_a, w2, w1, 0, (ways, True, part_b, target[half:])
    )
    back_b, slope_b, curv_b, grad_a = backward_half(
        n, err_b, hidden_b, w2, w1, 1, (ways, False, back_a, inverse)
    )
    grad_b = (scatter(back_b).astype(jnp.float32) / spectral).astype(jnp.bfloat16)
    curvature = spectral * sum_wide(jnp.sum(curv_a + curv_b), ways, 6)
    grad_out = tile_grad(
        flat_rows, flat_count, err_a, err_b, active_a, active_b, weight_out.shape, False, "grad_out"
    )
    raw_in = tile_grad(
        flat_rows, flat_count, x_a, x_b, slope_a, slope_b, weight_in.shape, True, "raw_in"
    )
    outer = jnp.einsum("jsk,jn->jskn", chosen, image) * mask_full
    grad_in = raw_in / spectral - (curvature / (spectral**3 * norm_probe) * outer)[:, None]
    outputs = jnp.concatenate([out_a, out_b], axis=0)
    token_grad = jnp.concatenate([grad_a, grad_b], axis=0)
    return (outputs, token_grad, grad_in, grad_out)


def solution(mesh):
    in_specs = (
        P("wide", "blk"),
        P("wide", "blk"),
        P("blk"),
        P("wide", "blk", None, None, None),
        P("wide", "blk", None, None, None),
        P("wide", "blk", None),
        P("wide", "blk"),
    )
    out_specs = (
        P("wide", "blk"),
        P("wide", "blk"),
        P("wide", "blk", None, None, None),
        P("wide", "blk", None, None, None),
    )
    return jax.shard_map(
        functools.partial(body, mesh.shape["blk"], mesh.shape["wide"]),
        mesh=mesh,
        in_specs=in_specs,
        out_specs=out_specs,
        check_vma=False,
    )
```
